256 devices in a mesh: rows: 64 (over z, x, core), cols: 4 (over y).
Axes of the slice: x: 4, y: 4, z: 8, core: 2. Of those that a mesh axis runs over, the one named last changes fastest.
Arguments:
- vectors: bfloat16 [64, 1048576], P('cols', 'rows'), may hold values from -110 to 110
- tile_vals: bfloat16 [12288, 256, 256], P('rows'), may hold values from -0.21875 to 0.21875
- tile_row: int32 [64, 192], P('rows'), may hold values from 0 to 63
- tile_src: int32 [64, 192], P('rows'), may hold values from 0 to 191, each once within a row
- send_list: int32 [4096, 2], P('rows'), may hold values from 0 to 63
- ritz_matrix: bfloat16 [64, 64], P(None, 'cols'), may hold values from -0.75 to 0.75
Outputs:
- rotated: bfloat16 [64, 1048576], P('cols', 'rows')
- gram_matrix: float32 [64, 64], P('cols')
- projected: float32 [64, 64], P('cols')
The draws below stay inside these ranges and needn't reach their ends.
Inputs may be any that keep to these rules, and one draw needn't show every extreme that they name: Each row of tile_src holds every number once, so that each own or received block is read by exactly one tile.
All inputs are finite; a program needn't handle non-finite values.
Results may differ from the reference program's by a relative error of at most 0.0062.
Values may be sent and summed in bfloat16 or wider, within the bound.
A program may use at most 128 MiB of HBM per device.

```python
import math
import jax
import jax.numpy as jnp
import numpy as np
from jax import lax

B = 256
K = 64
BR_DEV = 64
SLOT = 2
TILES_DEV = 192
TILES = 12288
NODES = 1048576
N_ROWS = 64


def draw_vectors(key, part):
    key_a, key_b, key_c = jax.random.split(key, 3)
    col_scale = jnp.exp(jax.random.uniform(key_a, (K, 1), minval=-1.15, maxval=1.15))
    node_scale = jnp.exp(jax.random.uniform(key_b, (1, NODES), minval=-1.15, maxval=1.15))
    position_scale = jnp.exp(math.log(3.0) * (jnp.arange(NODES, dtype=jnp.float32)[None, :] / NODES - 0.5))
    base_value = jnp.clip(jax.random.normal(key_c, (K, NODES)), -6.0, 6.0)
    return (base_value * col_scale * node_scale * position_scale).astype(jnp.bfloat16)


def place_ends(array, rng, least, largest):
    index_at = [jax.random.randint(jax.random.fold_in(rng, axis), (), 0, length) for axis, length in enumerate(array.shape)]
    longest = array.shape.index(max(array.shape))
    beside = index_at[:longest] + [(index_at[longest] + 1) % array.shape[longest]] + index_at[longest + 1:]
    return array.at[tuple(index_at)].set(least).at[tuple(beside)].set(largest)


def shard_levels(rng, extent, pieces, smallest, high):
    factor_of = 1.0
    for axis_at, blocks in pieces:
        draws = jax.random.uniform(jax.random.fold_in(jax.random.fold_in(rng, 6), axis_at), (blocks,), jnp.float32, smallest / len(pieces), high / len(pieces))
        factor_of = factor_of * jnp.repeat(jnp.exp(draws), extent[axis_at] // blocks).reshape((-1,) + (1,) * (len(extent) - 1 - axis_at))
    return factor_of


def rank_table(amount, slope):
    portions = [(1 << 20) // math.isqrt(standing ** slope) + 1 for standing in range(1, amount + 1)]
    width = 1 + sum(portions) // (1 << 30)
    return np.cumsum(np.array([max(1, weight // width) for weight in portions]))


def ranked_ids(stream_key, shape, amount, skew):
    table = rank_table(amount, skew)
    ticket = jax.random.randint(jax.random.fold_in(stream_key, 1), shape, 0, int(table[amount - 1]))
    rank = jnp.searchsorted(jnp.asarray(table, jnp.int32), ticket, side="right")
    return jax.random.permutation(jax.random.fold_in(stream_key, 2), amount)[rank].astype(jnp.int32)


def scatter_about(key, dims, spread, reach, shards=(), kind=jnp.bfloat16):
    array = spread * jax.random.normal(key, dims, jnp.float32)
    if shards:
        array = array * shard_levels(key, dims, shards, -0.22, 0.18)
    return jnp.clip(array, -reach, reach).astype(kind)


def setup_inputs(seed: int = 0) -> dict:
    seeds = jax.random.split(jax.random.key(seed), 7)
    return {
        "vectors": draw_vectors(jax.random.fold_in(seeds[6], 71), 0),
        "tile_vals": scatter_about(seeds[1], (TILES, B, B), (3 * B) ** -0.5, 0.21875, ((0, 64),)),
        "tile_row": place_ends(ranked_ids(seeds[2], (N_ROWS, TILES_DEV), BR_DEV, 2), jax.random.fold_in(seeds[2], 3), 0, BR_DEV - 1).astype(jnp.int32),
        "tile_src": jax.vmap(lambda own: jax.random.permutation(own, TILES_DEV))(jax.random.split(seeds[3], N_ROWS)).reshape((N_ROWS, TILES_DEV)).astype(jnp.int32),
        "send_list": place_ends(jax.random.randint(seeds[4], (N_ROWS * N_ROWS, SLOT), 0, BR_DEV), jax.random.fold_in(seeds[4], 1), 0, BR_DEV - 1).astype(jnp.int32),
        "ritz_matrix": scatter_about(seeds[5], (K, K), K ** -0.5, 0.75, ((1, 4),)),
    }


def apply_operator(vectors, tile_vals, tile_row, tile_src, send_list):
    columns = vectors.shape[0]
    blocked = vectors.reshape(columns, N_ROWS, BR_DEV, B)
    routes = send_list.reshape(N_ROWS, N_ROWS, SLOT)
    peer_ids = jnp.arange(N_ROWS, dtype=jnp.int32)
    block_ids = jnp.arange(BR_DEV, dtype=jnp.int32)

    def one_device(device):
        own_blocks = lax.dynamic_index_in_dim(blocked, device, 1, keepdims=False)
        wanted = lax.dynamic_index_in_dim(routes, device, 1, keepdims=False)
        incoming = blocked[:, peer_ids[:, None], wanted, :].reshape(columns, N_ROWS * SLOT, B)
        sources = jnp.concatenate([own_blocks, incoming], axis=1)
        tile_block = lax.dynamic_slice_in_dim(tile_vals, device * TILES_DEV, TILES_DEV, 0)
        row_ids = lax.dynamic_index_in_dim(tile_row, device, 0, keepdims=False)
        src_ids = lax.dynamic_index_in_dim(tile_src, device, 0, keepdims=False)
        chosen = jnp.take(sources, src_ids, axis=1).astype(jnp.float32)
        products = jnp.einsum("ktc,trc->ktr", chosen, tile_block.astype(jnp.float32), precision=lax.Precision.HIGHEST)
        onehot = (row_ids[None, :] == block_ids[:, None]).astype(jnp.float32)
        return jnp.einsum("bt,ktr->kbr", onehot, products, precision=lax.Precision.HIGHEST)

    stacked = lax.map(one_device, peer_ids)
    return jnp.transpose(stacked, (1, 0, 2, 3)).reshape(columns, NODES)


def reference(vectors, tile_vals, tile_row, tile_src, send_list, ritz_matrix):
    first_pass = apply_operator(vectors, tile_vals, tile_row, tile_src, send_list).astype(jnp.bfloat16)
    second = apply_operator(first_pass, tile_vals, tile_row, tile_src, send_list)
    filtered = (2.0 * second - vectors.astype(jnp.float32)).astype(jnp.bfloat16)
    operated = apply_operator(filtered, tile_vals, tile_row, tile_src, send_list).astype(jnp.bfloat16)
    gram_matrix = jnp.dot(filtered, filtered.T, preferred_element_type=jnp.float32) / NODES
    projected = jnp.dot(operated, filtered.T, preferred_element_type=jnp.float32) / NODES
    rotated = jnp.dot(ritz_matrix.T, filtered, preferred_element_type=jnp.float32).astype(jnp.bfloat16)
    return (rotated, gram_matrix, projected)
```

```python
import functools

import jax
import jax.numpy as jnp
from jax import lax
from jax.experimental import pallas as pl
from jax.experimental.pallas import tpu as pltpu
from jax.sharding import PartitionSpec as P

MESH = pl.DeviceIdType.MESH
F32, BF16 = jnp.float32, jnp.bfloat16
X, C = 4, 2
HV = 8
CH = 4
DIMS = dict(x=X, c=C)


def unrolled(count, unroll, step):
    assert count % unroll == 0

    def body(i, carry):
        for u in range(unroll):
            step(i * unroll + u)
        return carry

    lax.fori_loop(0, count // unroll, body, 0)


def kernel(
    n, ny, nb, nt, total_nodes,
    inv_ref, slot_ref, same_ref, last_ref, send_ref, vec_ref, ritz_ref, tiles_hbm,
    rot_ref, gram_ref, proj_ref,
    tiles, cur, outb, land, prods, accs, opb, full, red1, red2,
    tile_sem, ssem, rsem, ysend, yrecv, qsend, qrecv,
):
    Z = n // (X * C)
    me, cy = lax.axis_index("rows"), lax.axis_index("cols")
    z, x, c = lax.div(me, X * C), lax.rem(lax.div(me, C), X), lax.rem(me, C)
    ntc = nt // tile_sem.shape[0]
    per = n // CH

    def split(k):
        return lax.rem(k, Z), lax.rem(lax.div(k, Z), X), lax.div(k, Z * X)

    def target(k):
        dz, dx, dc = split(k)
        return (lax.rem(z + dz, Z) * X + lax.rem(x + dx, X)) * C + lax.rem(c + dc, C)

    def origin(k):
        dz, dx, dc = split(k)
        return (lax.rem(z - dz + Z, Z) * X + lax.rem(x - dx + X, X)) * C + lax.rem(c - dc + C, C)

    loads = [
        pltpu.make_async_copy(
            tiles_hbm.at[pl.ds(i * ntc, ntc)], tiles.at[pl.ds(i * ntc, ntc)], tile_sem.at[i]
        )
        for i in range(tile_sem.shape[0])
    ]
    for load in loads:
        load.start()

    barrier = pltpu.get_barrier_semaphore()

    def greet(k, carry):
        pl.semaphore_signal(barrier, inc=1, device_id={"rows": target(k)}, device_id_type=MESH)
        return carry

    lax.fori_loop(1, n, greet, 0)
    for d in range(1, ny):
        pl.semaphore_signal(
            barrier, inc=1, device_id={"cols": lax.rem(cy + d, ny)}, device_id_type=MESH
        )

    def unpack(r):
        both = vec_ref[:, pl.ds(pl.multiple_of(r * 256, 256), 256)].astype(F32)
        cur[0, 0, r] = both[:HV]
        cur[0, 1, r] = both[HV:]

    unrolled(nb, 8, unpack)

    def chosen(side, h, dest):
        return jnp.concatenate(
            [cur[side, h, send_ref[dest, 0]], cur[side, h, send_ref[dest, 1]]], axis=0
        ).astype(BF16)

    def pack(p, h):
        side = p % 2
        land[p, h, 0] = chosen(side, h, me)

        def step(k):
            outb[p, h, k] = chosen(side, h, target(k))

        unrolled(n, 8, step)

    def message(p, h, k, dest):
        return pltpu.make_async_remote_copy(
            src_ref=outb.at[p, h, k], dst_ref=land.at[p, h, k],
            send_sem=ssem.at[p, h], recv_sem=rsem.at[p, h, lax.div(k, per)],
            device_id={"rows": dest}, device_id_type=MESH,
        )

    def send(p, h):
        def step(k, carry):
            message(p, h, k, target(k)).start()
            return carry

        lax.fori_loop(1, n, step, 0)

    def arrived(p, h, g):
        low = max(1, g * per)
        count = (g + 1) * per - low
        pltpu.make_async_remote_copy(
            src_ref=outb.at[p, h, pl.ds(low, count)], dst_ref=land.at[p, h, pl.ds(low, count)],
            send_sem=ssem.at[p, h], recv_sem=rsem.at[p, h, g],
            device_id={"rows": target(1)}, device_id_type=MESH,
        ).wait_recv()

    def sent(p, h):
        pltpu.make_async_remote_copy(
            src_ref=outb.at[p, h, pl.ds(1, n - 1)], dst_ref=land.at[p, h, pl.ds(1, n - 1)],
            send_sem=ssem.at[p, h], recv_sem=rsem.at[p, h, 0],
            device_id={"rows": target(1)}, device_id_type=MESH,
        ).wait_send()

    def product(rows, tile):
        return lax.dot_general(
            rows, tiles[tile], (((1,), (1,)), ((), ())), preferred_element_type=F32
        )

    def own_products(p, h):
        def step(s):
            prods[h, s] = product(cur[p % 2, h, s].astype(BF16), inv_ref[s])

        unrolled(nb, 8, step)

    def received_products(p, h):
        for g in range(CH):
            arrived(p, h, g)

            def step(i):
                k = g * per + i
                s = nb + 2 * origin(k)
                block = land[p, h, k]
                prods[h, s] = product(block, inv_ref[s])[:HV]
                prods[h, s + 1] = product(block, inv_ref[s + 1])[HV:]

            unrolled(per, 4, step)

    def combine(h, emit):
        def add(i, total):
            for u in range(8):
                k = i * 8 + u
                total = total * same_ref[k] + prods[h, slot_ref[k]]
                accs[k] = total
            return total

        lax.fori_loop(0, nt // 8, add, jnp.zeros((HV, 256), F32))

        def pair(i):
            emit(i, accs[last_ref[2 * i]], accs[last_ref[2 * i + 1]])

        unrolled(nb // 2, 4, pair)

    def across(h, d):
        return pltpu.make_async_remote_copy(
            src_ref=full.at[cy, h], dst_ref=full.at[cy, h],
            send_sem=ysend.at[h, d - 1], recv_sem=yrecv.at[h, d - 1],
            device_id={"cols": lax.rem(cy + d, ny)}, device_id_type=MESH,
        )

    def across_arrival(h, d):
        slot = lax.rem(cy - d + ny, ny)
        return pltpu.make_async_remote_copy(
            src_ref=full.at[slot, h], dst_ref=full.at[slot, h],
            send_sem=ysend.at[h, d - 1], recv_sem=yrecv.at[h, d - 1],
            device_id={"cols": lax.rem(cy + d, ny)}, device_id_type=MESH,
        )

    accs[nt] = jnp.zeros((HV, 256), F32)
    pack(0, 0)
    pl.semaphore_wait(barrier, n - 1 + ny - 1)
    send(0, 0)
    pack(0, 1)
    send(0, 1)
    for load in loads:
        load.wait()

    def first(h):
        def emit(i, a, b):
            cur[1, h, 2 * i] = a.astype(BF16).astype(F32)
            cur[1, h, 2 * i + 1] = b.astype(BF16).astype(F32)

        return emit

    def second(h):
        def emit(i, a, b):
            old = vec_ref[:, pl.ds(pl.multiple_of(i * 512, 512), 512)].astype(F32)
            old = old[h * HV : (h + 1) * HV]
            both = jnp.concatenate([2.0 * a - old[:, :256], 2.0 * b - old[:, 256:]], axis=0)
            both = both.astype(BF16)
            full[cy, h, i] = both
            both = both.astype(F32)
            cur[0, h, 2 * i] = both[:HV]
            cur[0, h, 2 * i + 1] = both[HV:]

        return emit

    def third(h):
        def emit(i, a, b):
            opb[h, i] = jnp.concatenate([a, b], axis=0).astype(BF16)

        return emit

    for p, maker in ((0, first), (1, second)):
        for h in (0, 1):
            own_products(p, h)
            received_products(p, h)
            combine(h, maker(h))
            pack(p + 1, h)
            send(p + 1, h)
            if p == 1:
                for d in range(1, ny):
                    across(h, d).start()

    own_products(2, 0)
    own_products(2, 1)
    received_products(2, 0)
    combine(0, third(0))

    wide = ny * 2 * 2 * HV
    narrow = ny * 2 * HV
    column = lax.broadcasted_iota(jnp.int32, (narrow, wide), 1)
    vector = lax.broadcasted_iota(jnp.int32, (narrow, wide), 0)
    matches = lax.div(column, 32) * 16 + lax.rem(lax.div(column, 16), 2) * 8 + lax.rem(column, 8) == vector
    parity = lax.rem(lax.div(column, 8), 2)
    ritz = ritz_ref[...]
    turns = [
        lax.dot_general(
            ritz, jnp.where(matches & (parity == q), 1.0, 0.0).astype(BF16),
            (((0,), (0,)), ((), ())), preferred_element_type=F32,
        )
        for q in (0, 1)
    ]
    turn = jnp.concatenate(turns, axis=0).astype(BF16)

    for h in (0, 1):
        for d in range(1, ny):
            across_arrival(h, d).wait_recv()

    def weights(i):
        return full[:, :, i].reshape(wide, 256)

    def contract(rows, i):
        return lax.dot_general(
            rows, weights(i), (((1,), (1,)), ((), ())), preferred_element_type=F32
        )

    def beside(j, total):
        for u in range(4):
            i = j * 4 + u
            both = jnp.concatenate([full[cy, 0, i], full[cy, 1, i], opb[0, i]], axis=0)
            total = total + contract(both, i)
            turned = jnp.dot(turn, weights(i), preferred_element_type=F32).astype(BF16)
            at = pl.multiple_of(i * 512, 512)
            rot_ref[:, pl.ds(at, 256)] = turned[: 2 * HV]
            rot_ref[:, pl.ds(at + 256, 256)] = turned[2 * HV :]
        return total

    early = lax.fori_loop(0, nb // 8, beside, jnp.zeros((6 * HV, wide), F32))

    received_products(2, 1)
    combine(1, third(1))

    def ending(j, total):
        for u in range(4):
            i = j * 4 + u
            total = total + contract(opb[1, i], i)
        return total

    late = lax.fori_loop(0, nb // 8, ending, jnp.zeros((2 * HV, wide), F32))
    sums = jnp.concatenate([early, late], axis=0).reshape(4, 2, HV, wide)
    odd = lax.rem(lax.div(lax.broadcasted_iota(jnp.int32, (4, HV, wide), 2), 8), 2) == 1
    sums = jnp.where(odd, sums[:, 1], sums[:, 0]).reshape(4 * HV, wide)
    picked = lax.dot_general(
        sums, jnp.where(matches, 1.0, 0.0).astype(F32), (((1,), (1,)), ((), ())),
        precision=lax.Precision.HIGHEST, preferred_element_type=F32,
    )
    mine = jnp.concatenate([picked[: 2 * HV], picked[2 * HV :]], axis=1)

    def reduce(stage, red, mine, position, count, to):
        red[position] = mine

        def copies(d, slot):
            return pltpu.make_async_remote_copy(
                src_ref=red.at[slot], dst_ref=red.at[slot],
                send_sem=qsend.at[stage, d - 1], recv_sem=qrecv.at[stage, d - 1],
                device_id={"rows": to(d)}, device_id_type=MESH,
            )

        for d in range(1, count):
            copies(d, position).start()
        for d in range(1, count):
            copies(d, lax.rem(position - d + count, count)).wait_recv()
        total = red[0]
        for d in range(1, count):
            total = total + red[d]
        for d in range(1, count):
            copies(d, position).wait_send()
        return total

    plane = X * C
    spot = lax.rem(me, plane)
    mine = reduce(0, red1, mine, spot, plane, lambda d: z * plane + lax.rem(spot + d, plane))
    mine = reduce(1, red2, mine, z, Z, lambda d: lax.rem(z + d, Z) * plane + spot)
    mine = mine * (1.0 / total_nodes)
    gram_ref[...] = mine[:, :narrow]
    proj_ref[...] = mine[:, narrow:]
    for p in range(3):
        for h in (0, 1):
            sent(p, h)
    for h in (0, 1):
        for d in range(1, ny):
            across(h, d).wait_send()


def orders(tile_row, tile_src, nb):
    row, src = tile_row.reshape(-1), tile_src.reshape(-1)
    nt = row.shape[0]
    at = jnp.arange(nt, dtype=jnp.int32)
    inverse = jnp.sum(jnp.where(src[:, None] == at[None, :], at[:, None], 0), axis=0)
    key = row * nt + at
    rank = jnp.sum((key[None, :] < key[:, None]).astype(jnp.int32), axis=1)
    placed = rank[:, None] == at[None, :]
    slot = jnp.sum(jnp.where(placed, src[:, None], 0), axis=0)
    rows = jnp.sum(jnp.where(placed, row[:, None], 0), axis=0)
    before = jnp.sum(jnp.where(rank[:, None] + 1 == at[None, :], row[:, None] + 1, 0), axis=0) - 1
    same = (rows == before).astype(F32)
    blocks = jnp.arange(nb, dtype=jnp.int32)
    upto = jnp.sum((row[:, None] <= blocks[None, :]).astype(jnp.int32), axis=0)
    under = jnp.sum((row[:, None] < blocks[None, :]).astype(jnp.int32), axis=0)
    last = jnp.where(upto > under, upto - 1, nt)
    return inverse, slot, same, last


def solution(mesh):
    n, ny = mesh.shape["rows"], mesh.shape["cols"]

    def body(vectors, tile_vals, tile_row, tile_src, send_list, ritz):
        nt = tile_vals.shape[0]
        nb = vectors.shape[1] // 256
        k = ritz.shape[0]
        inverse, slot, same, last = orders(tile_row, tile_src, nb)
        smem = pl.BlockSpec(memory_space=pltpu.SMEM)
        vmem = pl.BlockSpec(memory_space=pltpu.VMEM)
        dma = pltpu.SemaphoreType.DMA
        return pl.pallas_call(
            functools.partial(kernel, n, ny, nb, nt, vectors.shape[1] * n),
            out_shape=(
                jax.ShapeDtypeStruct(vectors.shape, BF16),
                jax.ShapeDtypeStruct((2 * HV, k), F32),
                jax.ShapeDtypeStruct((2 * HV, k), F32),
            ),
            in_specs=[smem] * 5 + [vmem] * 2 + [pl.BlockSpec(memory_space=pl.ANY)],
            out_specs=(vmem, vmem, vmem),
            scratch_shapes=[
                pltpu.VMEM((nt, 256, 256), BF16),
                pltpu.VMEM((2, 2, nb, HV, 256), F32),
                pltpu.VMEM((3, 2, n, 2 * HV, 256), BF16),
                pltpu.VMEM((3, 2, n, 2 * HV, 256), BF16),
                pltpu.VMEM((2, nt, HV, 256), F32),
                pltpu.VMEM((nt + 1, HV, 256), F32),
                pltpu.VMEM((2, nb // 2, 2 * HV, 256), BF16),
                pltpu.VMEM((ny, 2, nb // 2, 2 * HV, 256), BF16),
                pltpu.VMEM((X * C, 2 * HV, 2 * k), F32),
                pltpu.VMEM((n // (X * C), 2 * HV, 2 * k), F32),
                dma((8,)),
                dma((3, 2)),
                dma((3, 2, CH)),
                dma((2, ny - 1)),
                dma((2, ny - 1)),
                dma((2, 7)),
                dma((2, 7)),
            ],
            compiler_params=pltpu.CompilerParams(
                collective_id=0, has_side_effects=True, vmem_limit_bytes=56 << 20
            ),
        )(inverse, slot, same, last, send_list, vectors, ritz, tile_vals)

    return jax.shard_map(
        body,
        mesh=mesh,
        in_specs=(
            P("cols", "rows"),
            P("rows", None, None),
            P("rows", None),
            P("rows", None),
            P("rows", None),
            P(None, "cols"),
        ),
        out_specs=(P("cols", "rows"), P("cols", None), P("cols", None)),
        check_vma=False,
    )
```

```python
import functools

import jax
import jax.numpy as jnp
from jax import lax
from jax.experimental import pallas as pl
from jax.experimental.pallas import tpu as pltpu
from jax.sharding import PartitionSpec as P

MESH = pl.DeviceIdType.MESH
F32, BF16 = jnp.float32, jnp.bfloat16
X, C = 4, 2
HV = 8
CH = 4
DIMS = dict(x=X, c=C)


def unrolled(count, unroll, step):
    assert count % unroll == 0

    def body(i, carry):
        for u in range(unroll):
            step(i * unroll + u)
        return carry

    lax.fori_loop(0, count // unroll, body, 0)


def kernel(
    n, ny, nb, nt, total_nodes,
    row_ref, src_ref, send_ref, ritz_ref, vec_hbm, tiles_hbm,
    rot_ref, sums_ref,
    vec_ref, tiles, cur, outb, land, prods, accs, opb, full, red1, red2,
    index_v, same_v, index_s, same_s,
    vec_sem, index_sem, tile_sem, ssem, rsem, ysend, yrecv, qsend, qrecv,
):
    Z = n // (X * C)
    me, cy = lax.axis_index("rows"), lax.axis_index("cols")
    z, x, c = lax.div(me, X * C), lax.rem(lax.div(me, C), X), lax.rem(me, C)
    ntc = nt // tile_sem.shape[0]
    per = n // CH

    def split(k):
        return lax.rem(k, Z), lax.rem(lax.div(k, Z), X), lax.div(k, Z * X)

    def target(k):
        dz, dx, dc = split(k)
        return (lax.rem(z + dz, Z) * X + lax.rem(x + dx, X)) * C + lax.rem(c + dc, C)

    def origin(k):
        dz, dx, dc = split(k)
        return (lax.rem(z - dz + Z, Z) * X + lax.rem(x - dx + X, X)) * C + lax.rem(c - dc + C, C)

    loads = [
        pltpu.make_async_copy(
            tiles_hbm.at[pl.ds(i * ntc, ntc)], tiles.at[pl.ds(i * ntc, ntc)], tile_sem.at[i]
        )
        for i in range(tile_sem.shape[0])
    ]
    bring = pltpu.make_async_copy(vec_hbm, vec_ref, vec_sem)
    bring.start()
    zs = [lax.rem(z + d, Z) * (X * C) for d in range(Z)]

    barrier = pltpu.get_barrier_semaphore()

    def each_peer(act):
        def plane(g, carry, first=0):
            dx, dc = lax.rem(g, X), lax.div(g, X)
            rest = lax.rem(x + dx, X) * C + lax.rem(c + dc, C)
            for d in range(first, Z):
                act(g * Z + d, zs[d] + rest)
            return carry

        plane(0, 0, 1)
        lax.fori_loop(1, X * C, plane, 0)

    each_peer(
        lambda k, dest: pl.semaphore_signal(
            barrier, inc=1, device_id={"rows": dest}, device_id_type=MESH
        )
    )
    for d in range(1, ny):
        pl.semaphore_signal(
            barrier, inc=1, device_id={"cols": lax.rem(cy + d, ny)}, device_id_type=MESH
        )

    def unpack(r):
        both = vec_ref[:, pl.ds(pl.multiple_of(r * 256, 256), 256)].astype(F32)
        cur[0, 0, r] = both[:HV]
        cur[0, 1, r] = both[HV:]

    bring.wait()
    for load in loads:
        load.start()
    unrolled(nb, 8, unpack)

    def chosen(side, h, dest):
        return jnp.concatenate(
            [cur[side, h, send_ref[0, dest]], cur[side, h, send_ref[1, dest]]], axis=0
        ).astype(BF16)

    def pack(p, h):
        side = p % 2
        land[p, h, 0] = chosen(side, h, me)

        def step(k, dest):
            outb[p, h, k] = chosen(side, h, dest)

        each_peer(step)

    def message(p, h, k, dest):
        return pltpu.make_async_remote_copy(
            src_ref=outb.at[p, h, k], dst_ref=land.at[p, h, k],
            send_sem=ssem.at[p, h], recv_sem=rsem.at[p, h, lax.div(k, per)],
            device_id={"rows": dest}, device_id_type=MESH,
        )

    def send(p, h):
        each_peer(lambda k, dest: message(p, h, k, dest).start())

    def arrived(p, h, g):
        low = max(1, g * per)
        count = (g + 1) * per - low
        pltpu.make_async_remote_copy(
            src_ref=outb.at[p, h, pl.ds(low, count)], dst_ref=land.at[p, h, pl.ds(low, count)],
            send_sem=ssem.at[p, h], recv_sem=rsem.at[p, h, g],
            device_id={"rows": target(1)}, device_id_type=MESH,
        ).wait_recv()

    def sent(p, h):
        pltpu.make_async_remote_copy(
            src_ref=outb.at[p, h, pl.ds(1, n - 1)], dst_ref=land.at[p, h, pl.ds(1, n - 1)],
            send_sem=ssem.at[p, h], recv_sem=rsem.at[p, h, 0],
            device_id={"rows": target(1)}, device_id_type=MESH,
        ).wait_send()

    def product(rows, tile):
        return lax.dot_general(
            rows, tiles[tile], (((1,), (0,)), ((), ())), preferred_element_type=F32
        )

    def own_products(p, h):
        def step(s):
            prods[h, s] = product(cur[p % 2, h, s].astype(BF16), index_s[0, s])

        unrolled(nb, 8, step)

    def received_products(p, h, g):
        arrived(p, h, g)

        def step(i):
            k = g * per + i
            s = nb + 2 * origin(k)
            block = land[p, h, k]
            prods[h, s] = product(block, index_s[0, s])[:HV]
            prods[h, s + 1] = product(block, index_s[0, s + 1])[HV:]

        unrolled(per, 4, step)

    def add(h, first, count):
        def step(i, total):
            for u in range(8):
                k = first + i * 8 + u
                total = total * same_s[0, k] + prods[h, index_s[1, k]]
                accs[k] = total
            return total

        lax.fori_loop(0, count // 8, step, jnp.zeros((HV, 256), F32))

    def apply(p, h):
        for g in range(CH):
            received_products(p, h, g)
            if g == CH // 2 - 1:
                add(h, 0, nb + n)
        add(h, nb + n, n)

    def summed(r):
        return accs[index_s[2, r]] + accs[index_s[2, nb + r]]

    def pairs(emit):
        unrolled(nb // 2, 4, lambda i: emit(i, summed(2 * i), summed(2 * i + 1)))

    def across(h, d):
        return pltpu.make_async_remote_copy(
            src_ref=full.at[cy, h], dst_ref=full.at[cy, h],
            send_sem=ysend.at[h, d - 1], recv_sem=yrecv.at[h, d - 1],
            device_id={"cols": lax.rem(cy + d, ny)}, device_id_type=MESH,
        )

    def across_arrival(h, d):
        slot = lax.rem(cy - d + ny, ny)
        return pltpu.make_async_remote_copy(
            src_ref=full.at[slot, h], dst_ref=full.at[slot, h],
            send_sem=ysend.at[h, d - 1], recv_sem=yrecv.at[h, d - 1],
            device_id={"cols": lax.rem(cy + d, ny)}, device_id_type=MESH,
        )

    accs[nt] = jnp.zeros((HV, 256), F32)
    pack(0, 0)
    pl.semaphore_wait(barrier, n - 1 + ny - 1)
    send(0, 0)
    pack(0, 1)
    send(0, 1)

    side = (nt, nt)
    down = lax.broadcasted_iota(jnp.int32, side, 0)
    along = lax.broadcasted_iota(jnp.int32, side, 1)

    def upright(line):
        spread = jnp.where(down == along, jnp.broadcast_to(line, side).astype(F32), 0.0)
        return jnp.sum(spread, axis=1, keepdims=True).astype(jnp.int32)

    def gather(where, value):
        return jnp.sum(jnp.where(where, value, 0), axis=0, keepdims=True)

    src = src_ref[...]
    late = (src >= nb) & (lax.rem(lax.div(src - nb, 2), C) != c)
    row = row_ref[...] + jnp.where(late, nb, 0)
    row_c, src_c = upright(row), upright(src)
    key = row * nt + lax.broadcasted_iota(jnp.int32, (1, nt), 1)
    key_c = row_c * nt + lax.broadcasted_iota(jnp.int32, (nt, 1), 0)
    rank_c = jnp.sum(
        jnp.where(key < key_c, 1.0, 0.0).astype(F32), axis=1, keepdims=True
    ).astype(jnp.int32)
    placed = rank_c == along
    index_v[0:1, :nt] = gather(src_c == along, down)
    index_v[1:2, :nt] = gather(placed, src_c)
    upto = gather(row_c <= along, 1)
    under = gather(row_c < along, 1)
    index_v[2:3, :nt] = jnp.where(upto > under, upto - 1, nt)
    same_v[0:1, :nt] = jnp.where(
        gather(placed, row_c) + 1 == gather(rank_c + 1 == along, row_c + 1), 1.0, 0.0
    )
    moves = [
        pltpu.make_async_copy(index_v, index_s, index_sem.at[0]),
        pltpu.make_async_copy(same_v, same_s, index_sem.at[1]),
    ]
    for move in moves:
        move.start()
    for i, load in enumerate(loads):
        load.wait()

        def flip(j, i=i):
            t = i * ntc + j
            tiles[t] = tiles[t].T

        unrolled(ntc, 4, flip)
    for move in moves:
        move.wait()
    own_products(0, 0)
    own_products(0, 1)

    def first(h):
        def emit(i, a, b):
            cur[1, h, 2 * i] = a.astype(BF16).astype(F32)
            cur[1, h, 2 * i + 1] = b.astype(BF16).astype(F32)

        return emit

    def second(h):
        def emit(i, a, b):
            old = vec_ref[:, pl.ds(pl.multiple_of(i * 512, 512), 512)].astype(F32)
            old = old[h * HV : (h + 1) * HV]
            both = jnp.concatenate([2.0 * a - old[:, :256], 2.0 * b - old[:, 256:]], axis=0)
            both = both.astype(BF16)
            full[cy, h, i] = both
            both = both.astype(F32)
            cur[0, h, 2 * i] = both[:HV]
            cur[0, h, 2 * i + 1] = both[HV:]

        return emit

    def third(i, a, b):
        opb[i] = jnp.concatenate([a, b], axis=0).astype(BF16)

    for p, maker in ((0, first), (1, second)):
        for h in (0, 1):
            apply(p, h)
            pairs(maker(h))
            pack(p + 1, h)
            send(p + 1, h)
            if p == 1:
                for d in range(1, ny):
                    across(h, d).start()
            own_products(p + 1, h)

    apply(2, 0)
    pairs(third)

    wide = ny * 2 * 2 * HV
    narrow = ny * 2 * HV
    column = lax.broadcasted_iota(jnp.int32, (narrow, wide), 1)
    vector = lax.broadcasted_iota(jnp.int32, (narrow, wide), 0)
    matches = lax.div(column, 32) * 16 + lax.rem(lax.div(column, 16), 2) * 8 + lax.rem(column, 8) == vector
    parity = lax.rem(lax.div(column, 8), 2)
    turns = [
        lax.dot_general(
            ritz_ref[...], jnp.where(matches & (parity == q), 1.0, 0.0).astype(BF16),
            (((1,), (0,)), ((), ())), preferred_element_type=F32,
        )
        for q in (0, 1)
    ]
    turn = jnp.concatenate(turns, axis=0).astype(BF16)

    apply(2, 1)

    for h in (0, 1):
        for d in range(1, ny):
            across_arrival(h, d).wait_recv()

    def weights(i):
        return full[:, :, i].reshape(wide, 256)

    def contract(j, total):
        for u in range(4):
            i = j * 4 + u
            rest = jnp.concatenate([summed(2 * i), summed(2 * i + 1)], axis=0).astype(BF16)
            rows = jnp.concatenate([full[cy, 0, i], full[cy, 1, i], opb[i], rest], axis=0)
            total = total + lax.dot_general(
                rows, weights(i), (((1,), (1,)), ((), ())), preferred_element_type=F32
            )
        return total

    sums = lax.fori_loop(0, nb // 8, contract, jnp.zeros((8 * HV, wide), F32))

    def rotate():
        def step(i):
            turned = jnp.dot(turn, weights(i), preferred_element_type=F32).astype(BF16)
            at = pl.multiple_of(i * 512, 512)
            rot_ref[:, pl.ds(at, 256)] = turned[: 2 * HV]
            rot_ref[:, pl.ds(at + 256, 256)] = turned[2 * HV :]

        unrolled(nb // 2, 4, step)

    sums = sums.reshape(4, 2, HV, wide)
    odd = lax.rem(lax.div(lax.broadcasted_iota(jnp.int32, (4, HV, wide), 2), 8), 2) == 1
    sums = jnp.where(odd, sums[:, 1], sums[:, 0]).reshape(4 * HV, wide)
    picked = lax.dot_general(
        sums, jnp.where(matches, 1.0, 0.0).astype(F32), (((1,), (1,)), ((), ())),
        precision=lax.Precision.HIGHEST, preferred_element_type=F32,
    )
    mine = jnp.concatenate([picked[: 2 * HV], picked[2 * HV :]], axis=1)

    def reduce(stage, red, mine, position, count, to, meanwhile):
        red[position] = mine

        def copies(d, slot):
            return pltpu.make_async_remote_copy(
                src_ref=red.at[slot], dst_ref=red.at[slot],
                send_sem=qsend.at[stage, d - 1], recv_sem=qrecv.at[stage, d - 1],
                device_id={"rows": to(d)}, device_id_type=MESH,
            )

        for d in range(1, count):
            copies(d, position).start()
        meanwhile()
        for d in range(1, count):
            copies(d, lax.rem(position - d + count, count)).wait_recv()
        total = red[0]
        for d in range(1, count):
            total = total + red[d]
        for d in range(1, count):
            copies(d, position).wait_send()
        return total

    plane = X * C
    spot = lax.rem(me, plane)
    mine = reduce(0, red1, mine, spot, plane, lambda d: z * plane + lax.rem(spot + d, plane), rotate)
    mine = reduce(1, red2, mine, z, Z, lambda d: lax.rem(z + d, Z) * plane + spot, lambda: None)
    mine = mine * (1.0 / total_nodes)
    sums_ref[...] = mine
    for p in range(3):
        for h in (0, 1):
            sent(p, h)
    for h in (0, 1):
        for d in range(1, ny):
            across(h, d).wait_send()


def finish(rot_ref, sums_ref, rotated_hbm, gram_ref, projected_ref, sem):
    rows = rot_ref.shape[1] // sem.shape[0]
    copies = [
        pltpu.make_async_copy(
            rot_ref.at[:, pl.ds(i * rows, rows)], rotated_hbm.at[:, pl.ds(i * rows, rows)], sem.at[i]
        )
        for i in range(sem.shape[0])
    ]
    for copy in copies:
        copy.start()
    k = gram_ref.shape[1]
    gram_ref[...] = sums_ref[:, :k]
    projected_ref[...] = sums_ref[:, k:]
    for copy in copies:
        copy.wait()


def solution(mesh):
    n, ny = mesh.shape["rows"], mesh.shape["cols"]

    def body(vectors, tile_vals, tile_row, tile_src, send_list, ritz):
        nt = tile_vals.shape[0]
        nb = vectors.shape[1] // 256
        k = ritz.shape[0]
        smem = pl.BlockSpec(memory_space=pltpu.SMEM)
        vmem = pl.BlockSpec(memory_space=pltpu.VMEM)
        dma = pltpu.SemaphoreType.DMA
        anywhere = pl.BlockSpec(memory_space=pl.ANY)
        rotated, sums = pl.pallas_call(
            functools.partial(kernel, n, ny, nb, nt, vectors.shape[1] * n),
            out_shape=(
                pltpu.VMEM(vectors.shape, BF16),
                pltpu.VMEM((2 * HV, 2 * k), F32),
            ),
            in_specs=[vmem, vmem, smem, vmem, anywhere, anywhere],
            out_specs=(vmem, vmem),
            scratch_shapes=[
                pltpu.VMEM(vectors.shape, BF16),
                pltpu.VMEM((nt, 256, 256), BF16),
                pltpu.VMEM((2, 2, nb, HV, 256), F32),
                pltpu.VMEM((3, 2, n, 2 * HV, 256), BF16),
                pltpu.VMEM((3, 2, n, 2 * HV, 256), BF16),
                pltpu.VMEM((2, nt, HV, 256), F32),
                pltpu.VMEM((nt + 1, HV, 256), F32),
                pltpu.VMEM((nb // 2, 2 * HV, 256), BF16),
                pltpu.VMEM((ny, 2, nb // 2, 2 * HV, 256), BF16),
                pltpu.VMEM((X * C, 2 * HV, 2 * k), F32),
                pltpu.VMEM((n // (X * C), 2 * HV, 2 * k), F32),
                pltpu.VMEM((8, 256), jnp.int32),
                pltpu.VMEM((8, 256), F32),
                pltpu.SMEM((8, 256), jnp.int32),
                pltpu.SMEM((8, 256), F32),
                dma,
                dma((2,)),
                dma((8,)),
                dma((3, 2)),
                dma((3, 2, CH)),
                dma((2, ny - 1)),
                dma((2, ny - 1)),
                dma((2, 7)),
                dma((2, 7)),
            ],
            compiler_params=pltpu.CompilerParams(
                collective_id=0, has_side_effects=True, vmem_limit_bytes=56 << 20
            ),
        )(tile_row, tile_src, send_list.T, ritz.T, vectors, tile_vals)
        return pl.pallas_call(
            finish,
            out_shape=(
                jax.ShapeDtypeStruct(vectors.shape, BF16),
                jax.ShapeDtypeStruct((2 * HV, k), F32),
                jax.ShapeDtypeStruct((2 * HV, k), F32),
            ),
            in_specs=[vmem, vmem],
            out_specs=(anywhere, vmem, vmem),
            scratch_shapes=[dma((4,))],
            compiler_params=pltpu.CompilerParams(vmem_limit_bytes=4 << 20),
        )(rotated, sums)

    return jax.shard_map(
        body,
        mesh=mesh,
        in_specs=(
            P("cols", "rows"),
            P("rows", None, None),
            P("rows", None),
            P("rows", None),
            P("rows", None),
            P(None, "cols"),
        ),
        out_specs=(P("cols", "rows"), P("cols", None), P("cols", None)),
        check_vma=False,
    )
```

```python
import functools

import jax
import jax.numpy as jnp
from jax import lax
from jax.experimental import pallas as pl
from jax.experimental.pallas import tpu as pltpu
from jax.sharding import PartitionSpec as P

MESH = pl.DeviceIdType.MESH
F32, BF16 = jnp.float32, jnp.bfloat16
X, C = 4, 2
HV = 8


def unrolled(count, unroll, step):
    assert count % unroll == 0

    def body(i, carry):
        for u in range(unroll):
            step(i * unroll + u)
        return carry

    lax.fori_loop(0, count // unroll, body, 0)


def kernel(
    n, ny, nb, nt, total_nodes,
    row_hbm, src_hbm, send_hbm, ritz_hbm, vec_hbm, tiles_hbm,
    rot_ref, sums_ref,
    row_ref, src_ref, send_ref, ritz_ref, vec_ref, tiles, cur, outb, land, prods, accs, opb, full, red1, red2,
    index_v, same_v, index_s, same_s,
    small_sem, vec_sem, index_sem, tile_sem, ssem, rsem, ysend, yrecv, qsend, qrecv,
):
    Z = n // (X * C)
    me, cy = lax.axis_index("rows"), lax.axis_index("cols")
    z, x, c = lax.div(me, X * C), lax.rem(lax.div(me, C), X), lax.rem(me, C)
    ntc = nt // tile_sem.shape[0]
    far = sorted(range(Z), key=lambda d: -min(d, Z - d))
    groups = X * C

    def steps(g):
        return X - 1 - lax.rem(g, X), C - 1 - lax.div(g, X)

    loads = [
        pltpu.make_async_copy(
            tiles_hbm.at[pl.ds(i * ntc, ntc)], tiles.at[pl.ds(i * ntc, ntc)], tile_sem.at[i]
        )
        for i in range(tile_sem.shape[0])
    ]
    bring = pltpu.make_async_copy(vec_hbm, vec_ref, vec_sem)
    bring.start()
    pairs_in = ((send_hbm, send_ref), (row_hbm, row_ref), (src_hbm, src_ref), (ritz_hbm, ritz_ref))
    smalls = [pltpu.make_async_copy(a, b, small_sem.at[i]) for i, (a, b) in enumerate(pairs_in)]
    for small in smalls:
        small.start()
    to_z = [lax.rem(z + d, Z) * groups for d in far]
    from_z = [lax.rem(z - d + Z, Z) * groups for d in far]

    barrier = pltpu.get_barrier_semaphore()

    def each_peer(act):
        def plane(g, carry, count=Z):
            dx, dc = steps(g)
            rest = lax.rem(x + dx, X) * C + lax.rem(c + dc, C)
            for j in range(count):
                act(g * Z + j, to_z[j] + rest)
            return carry

        lax.fori_loop(0, groups - 1, plane, 0)
        plane(groups - 1, 0, Z - 1)

    each_peer(
        lambda k, dest: pl.semaphore_signal(
            barrier, inc=1, device_id={"rows": dest}, device_id_type=MESH
        )
    )
    for d in range(1, ny):
        pl.semaphore_signal(
            barrier, inc=1, device_id={"cols": lax.rem(cy + d, ny)}, device_id_type=MESH
        )

    def unpack(r):
        both = vec_ref[:, pl.ds(pl.multiple_of(r * 256, 256), 256)].astype(F32)
        cur[0, 0, r] = both[:HV]
        cur[0, 1, r] = both[HV:]

    bring.wait()
    for small in smalls:
        small.wait()
    for load in loads:
        load.start()
    unrolled(nb, 8, unpack)

    def chosen(side, h, dest):
        return jnp.concatenate(
            [cur[side, h, send_ref[0, dest]], cur[side, h, send_ref[1, dest]]], axis=0
        ).astype(BF16)

    def pack(p, h):
        side = p % 2
        land[p, h, n - 1] = chosen(side, h, me)

        def step(k, dest):
            outb[p, h, k] = chosen(side, h, dest)

        each_peer(step)

    def message(p, h, k, dest):
        return pltpu.make_async_remote_copy(
            src_ref=outb.at[p, h, k], dst_ref=land.at[p, h, k],
            send_sem=ssem.at[p, h], recv_sem=rsem.at[p, h, lax.div(k, Z)],
            device_id={"rows": dest}, device_id_type=MESH,
        )

    def send(p, h):
        each_peer(lambda k, dest: message(p, h, k, dest).start())

    def many(p, h, g, first, count):
        at = pl.ds(first, count)
        return pltpu.make_async_remote_copy(
            src_ref=outb.at[p, h, at], dst_ref=land.at[p, h, at],
            send_sem=ssem.at[p, h], recv_sem=rsem.at[p, h, g],
            device_id={"rows": lax.rem(me + 1, n)}, device_id_type=MESH,
        )

    def product(rows, tile):
        return lax.dot_general(
            rows, tiles[tile], (((1,), (0,)), ((), ())), preferred_element_type=F32
        )

    def own_products(p, h):
        def step(s):
            prods[h, s] = product(cur[p % 2, h, s].astype(BF16), index_s[0, s])

        unrolled(nb, 8, step)

    def received_products(p, h, g, count=Z):
        many(p, h, g, g * Z, count).wait_recv()
        dx, dc = steps(g)
        rest = lax.rem(x - dx + X, X) * C + lax.rem(c - dc + C, C)
        for j in range(Z):
            s = nb + 2 * (from_z[j] + rest)
            block = land[p, h, g * Z + j]
            prods[h, s] = product(block, index_s[0, s])[:HV]
            prods[h, s + 1] = product(block, index_s[0, s + 1])[HV:]

    def add(h, first, count):
        def step(i, total):
            for u in range(8):
                k = first + i * 8 + u
                total = total * same_s[0, k] + prods[h, index_s[1, k]]
                accs[k] = total
            return total

        lax.fori_loop(0, count // 8, step, jnp.zeros((HV, 256), F32))

    def apply(p, h):
        def step(g, carry):
            received_products(p, h, g)
            return carry

        lax.fori_loop(0, groups // 2, step, 0)
        add(h, 0, nb + n)
        lax.fori_loop(groups // 2, groups - 1, step, 0)
        received_products(p, h, groups - 1, Z - 1)
        add(h, nb + n, n)

    def summed(r):
        return accs[index_s[2, r]] + accs[index_s[2, nb + r]]

    def pairs(emit):
        unrolled(nb // 2, 4, lambda i: emit(i, summed(2 * i), summed(2 * i + 1)))

    def across(h, d):
        return pltpu.make_async_remote_copy(
            src_ref=full.at[cy, h], dst_ref=full.at[cy, h],
            send_sem=ysend.at[h, d - 1], recv_sem=yrecv.at[h, d - 1],
            device_id={"cols": lax.rem(cy + d, ny)}, device_id_type=MESH,
        )

    def across_arrival(h, d):
        slot = lax.rem(cy - d + ny, ny)
        return pltpu.make_async_remote_copy(
            src_ref=full.at[slot, h], dst_ref=full.at[slot, h],
            send_sem=ysend.at[h, d - 1], recv_sem=yrecv.at[h, d - 1],
            device_id={"cols": lax.rem(cy + d, ny)}, device_id_type=MESH,
        )

    accs[nt] = jnp.zeros((HV, 256), F32)
    pack(0, 0)
    pl.semaphore_wait(barrier, n - 1 + ny - 1)
    send(0, 0)
    pack(0, 1)
    send(0, 1)

    side = (nt, nt)
    down = lax.broadcasted_iota(jnp.int32, side, 0)
    along = lax.broadcasted_iota(jnp.int32, side, 1)

    def upright(line):
        spread = jnp.where(down == along, jnp.broadcast_to(line, side).astype(F32), 0.0)
        return jnp.sum(spread, axis=1, keepdims=True).astype(jnp.int32)

    def gather(where, value):
        return jnp.sum(jnp.where(where, value, 0), axis=0, keepdims=True)

    src = src_ref[...]
    late = (src >= nb) & (lax.rem(lax.div(src - nb, 2), C) == c)
    row = row_ref[...] + jnp.where(late, nb, 0)
    row_c, src_c = upright(row), upright(src)
    key = row * nt + lax.broadcasted_iota(jnp.int32, (1, nt), 1)
    key_c = row_c * nt + lax.broadcasted_iota(jnp.int32, (nt, 1), 0)
    rank_c = jnp.sum(
        jnp.where(key < key_c, 1.0, 0.0).astype(F32), axis=1, keepdims=True
    ).astype(jnp.int32)
    placed = rank_c == along
    index_v[0:1, :nt] = gather(src_c == along, down)
    index_v[1:2, :nt] = gather(placed, src_c)
    upto = gather(row_c <= along, 1)
    under = gather(row_c < along, 1)
    index_v[2:3, :nt] = jnp.where(upto > under, upto - 1, nt)
    same_v[0:1, :nt] = jnp.where(
        gather(placed, row_c) + 1 == gather(rank_c + 1 == along, row_c + 1), 1.0, 0.0
    )
    moves = [
        pltpu.make_async_copy(index_v, index_s, index_sem.at[0]),
        pltpu.make_async_copy(same_v, same_s, index_sem.at[1]),
    ]
    for move in moves:
        move.start()
    for i, load in enumerate(loads):
        load.wait()

        def flip(j, i=i):
            t = i * ntc + j
            tiles[t] = tiles[t].T

        unrolled(ntc, 4, flip)
    for move in moves:
        move.wait()
    own_products(0, 0)
    own_products(0, 1)

    def first(h):
        def emit(i, a, b):
            cur[1, h, 2 * i] = a.astype(BF16).astype(F32)
            cur[1, h, 2 * i + 1] = b.astype(BF16).astype(F32)

        return emit

    def second(h):
        def emit(i, a, b):
            old = vec_ref[:, pl.ds(pl.multiple_of(i * 512, 512), 512)].astype(F32)
            old = old[h * HV : (h + 1) * HV]
            both = jnp.concatenate([2.0 * a - old[:, :256], 2.0 * b - old[:, 256:]], axis=0)
            both = both.astype(BF16)
            full[cy, h, i] = both
            both = both.astype(F32)
            cur[0, h, 2 * i] = both[:HV]
            cur[0, h, 2 * i + 1] = both[HV:]

        return emit

    def third(i, a, b):
        opb[i] = jnp.concatenate([a, b], axis=0).astype(BF16)

    for p, maker in ((0, first), (1, second)):
        for h in (0, 1):
            apply(p, h)
            pairs(maker(h))
            pack(p + 1, h)
            send(p + 1, h)
            if p == 1:
                for d in range(1, ny):
                    across(h, d).start()
            own_products(p + 1, h)

    apply(2, 0)
    pairs(third)

    wide = ny * 2 * 2 * HV
    narrow = ny * 2 * HV
    column = lax.broadcasted_iota(jnp.int32, (narrow, wide), 1)
    vector = lax.broadcasted_iota(jnp.int32, (narrow, wide), 0)
    matches = lax.div(column, 32) * 16 + lax.rem(lax.div(column, 16), 2) * 8 + lax.rem(column, 8) == vector
    parity = lax.rem(lax.div(column, 8), 2)
    turns = [
        lax.dot_general(
            ritz_ref[...], jnp.where(matches & (parity == q), 1.0, 0.0).astype(BF16),
            (((1,), (0,)), ((), ())), preferred_element_type=F32,
        )
        for q in (0, 1)
    ]
    turn = jnp.concatenate(turns, axis=0).astype(BF16)

    apply(2, 1)

    for h in (0, 1):
        for d in range(1, ny):
            across_arrival(h, d).wait_recv()

    def weights(i):
        return full[:, :, i].reshape(wide, 256)

    def contract(j, total):
        for u in range(4):
            i = j * 4 + u
            rest = jnp.concatenate([summed(2 * i), summed(2 * i + 1)], axis=0).astype(BF16)
            rows = jnp.concatenate([full[cy, 0, i], full[cy, 1, i], opb[i], rest], axis=0)
            total = total + lax.dot_general(
                rows, weights(i), (((1,), (1,)), ((), ())), preferred_element_type=F32
            )
        return total

    sums = lax.fori_loop(0, nb // 8, contract, jnp.zeros((8 * HV, wide), F32))

    def rotate():
        def step(i):
            turned = jnp.dot(turn, weights(i), preferred_element_type=F32).astype(BF16)
            at = pl.multiple_of(i * 512, 512)
            rot_ref[:, pl.ds(at, 256)] = turned[: 2 * HV]
            rot_ref[:, pl.ds(at + 256, 256)] = turned[2 * HV :]

        unrolled(nb // 2, 4, step)

    sums = sums.reshape(4, 2, HV, wide)
    even, odd = sums[:, 0].reshape(4 * HV, wide), sums[:, 1].reshape(4 * HV, wide)
    first = lax.rem(lax.div(lax.broadcasted_iota(jnp.int32, (2 * HV, wide), 1), HV), 2) == 0
    mine = jnp.where(
        first,
        even[: 2 * HV] + pltpu.roll(odd[: 2 * HV], wide - HV, 1),
        odd[2 * HV :] + pltpu.roll(even[2 * HV :], HV, 1),
    )

    def reduce(stage, red, mine, position, count, to, meanwhile):
        red[position] = mine

        def copies(d, slot):
            return pltpu.make_async_remote_copy(
                src_ref=red.at[slot], dst_ref=red.at[slot],
                send_sem=qsend.at[stage, d - 1], recv_sem=qrecv.at[stage, d - 1],
                device_id={"rows": to(d)}, device_id_type=MESH,
            )

        for d in range(1, count):
            copies(d, position).start()
        meanwhile()
        for d in range(1, count):
            copies(d, lax.rem(position - d + count, count)).wait_recv()
        total = red[0]
        for d in range(1, count):
            total = total + red[d]
        for d in range(1, count):
            copies(d, position).wait_send()
        return total

    plane = X * C
    spot = lax.rem(me, plane)
    mine = reduce(0, red1, mine, spot, plane, lambda d: z * plane + lax.rem(spot + d, plane), rotate)
    mine = reduce(1, red2, mine, z, Z, lambda d: lax.rem(z + d, Z) * plane + spot, lambda: None)
    mine = mine * (1.0 / total_nodes)
    sums_ref[...] = mine
    for p in range(3):
        for h in (0, 1):
            many(p, h, 0, 0, n - 1).wait_send()
    for h in (0, 1):
        for d in range(1, ny):
            across(h, d).wait_send()


def finish(rot_ref, sums_ref, rotated_hbm, gram_ref, projected_ref, sem):
    rows = rot_ref.shape[1] // sem.shape[0]
    copies = [
        pltpu.make_async_copy(
            rot_ref.at[:, pl.ds(i * rows, rows)], rotated_hbm.at[:, pl.ds(i * rows, rows)], sem.at[i]
        )
        for i in range(sem.shape[0])
    ]
    for copy in copies:
        copy.start()
    wide, k = sums_ref.shape[1], gram_ref.shape[1]
    column = lax.broadcasted_iota(jnp.int32, (wide, k), 0)
    vector = lax.broadcasted_iota(jnp.int32, (wide, k), 1)
    place = lax.div(column, 2 * HV) * HV + lax.rem(column, HV) == vector
    parity = lax.rem(lax.div(column, HV), 2)
    for q, out_ref in ((0, gram_ref), (1, projected_ref)):
        out_ref[...] = jnp.dot(
            sums_ref[...], jnp.where(place & (parity == q), 1.0, 0.0).astype(F32),
            precision=lax.Precision.HIGHEST, preferred_element_type=F32,
        )
    for copy in copies:
        copy.wait()


def solution(mesh):
    n, ny = mesh.shape["rows"], mesh.shape["cols"]

    def body(vectors, tile_vals, tile_row, tile_src, send_list, ritz):
        nt = tile_vals.shape[0]
        nb = vectors.shape[1] // 256
        k = ritz.shape[0]
        vmem = pl.BlockSpec(memory_space=pltpu.VMEM)
        dma = pltpu.SemaphoreType.DMA
        anywhere = pl.BlockSpec(memory_space=pl.ANY)
        rotated, sums = pl.pallas_call(
            functools.partial(kernel, n, ny, nb, nt, vectors.shape[1] * n),
            out_shape=(
                pltpu.VMEM(vectors.shape, BF16),
                pltpu.VMEM((2 * HV, 2 * k), F32),
            ),
            in_specs=[anywhere] * 6,
            out_specs=(vmem, vmem),
            scratch_shapes=[
                pltpu.VMEM(tile_row.shape, jnp.int32),
                pltpu.VMEM(tile_src.shape, jnp.int32),
                pltpu.SMEM(send_list.shape[::-1], jnp.int32),
                pltpu.VMEM(ritz.shape[::-1], BF16),
                pltpu.VMEM(vectors.shape, BF16),
                pltpu.VMEM((nt, 256, 256), BF16),
                pltpu.VMEM((2, 2, nb, HV, 256), F32),
                pltpu.VMEM((3, 2, n, 2 * HV, 256), BF16),
                pltpu.VMEM((3, 2, n, 2 * HV, 256), BF16),
                pltpu.VMEM((2, nt, HV, 256), F32),
                pltpu.VMEM((nt + 1, HV, 256), F32),
                pltpu.VMEM((nb // 2, 2 * HV, 256), BF16),
                pltpu.VMEM((ny, 2, nb // 2, 2 * HV, 256), BF16),
                pltpu.VMEM((X * C, 2 * HV, 2 * k), F32),
                pltpu.VMEM((n // (X * C), 2 * HV, 2 * k), F32),
                pltpu.VMEM((8, 256), jnp.int32),
                pltpu.VMEM((8, 256), F32),
                pltpu.SMEM((8, 256), jnp.int32),
                pltpu.SMEM((8, 256), F32),
                dma((4,)),
                dma,
                dma((2,)),
                dma((8,)),
                dma((3, 2)),
                dma((3, 2, X * C)),
                dma((2, ny - 1)),
                dma((2, ny - 1)),
                dma((2, 7)),
                dma((2, 7)),
            ],
            compiler_params=pltpu.CompilerParams(
                collective_id=0, has_side_effects=True, vmem_limit_bytes=56 << 20
            ),
        )(tile_row, tile_src, send_list.T, ritz.T, vectors, tile_vals)
        return pl.pallas_call(
            finish,
            out_shape=(
                jax.ShapeDtypeStruct(vectors.shape, BF16),
                jax.ShapeDtypeStruct((2 * HV, k), F32),
                jax.ShapeDtypeStruct((2 * HV, k), F32),
            ),
            in_specs=[vmem, vmem],
            out_specs=(anywhere, vmem, vmem),
            scratch_shapes=[dma((4,))],
            compiler_params=pltpu.CompilerParams(vmem_limit_bytes=4 << 20),
        )(rotated, sums)

    return jax.shard_map(
        body,
        mesh=mesh,
        in_specs=(
            P("cols", "rows"),
            P("rows", None, None),
            P("rows", None),
            P("rows", None),
            P("rows", None),
            P(None, "cols"),
        ),
        out_specs=(P("cols", "rows"), P("cols", None), P("cols", None)),
        check_vma=False,
    )
```

```python
import functools

import jax
import jax.numpy as jnp
from jax import lax
from jax.experimental import pallas as pl
from jax.experimental.pallas import tpu as pltpu
from jax.sharding import PartitionSpec as P

MESH = pl.DeviceIdType.MESH
F32, BF16 = jnp.float32, jnp.bfloat16
X, C = 4, 2
HV = 8


def unrolled(count, unroll, step):
    assert count % unroll == 0

    def body(i, carry):
        for u in range(unroll):
            step(i * unroll + u)
        return carry

    lax.fori_loop(0, count // unroll, body, 0)


def kernel(
    n, ny, nb, nt, total_nodes,
    row_hbm, src_hbm, send_hbm, ritz_hbm, vec_hbm, tiles_hbm,
    rot_ref, sums_ref,
    row_ref, src_ref, send_ref, ritz_ref, vec_ref, tiles, cur, outb, land, prods, accs, opb, full, red1, red2,
    index_v, same_v, index_s, same_s,
    small_sem, vec_sem, index_sem, tile_sem, ssem, rsem, ysend, yrecv, qsend, qrecv,
):
    Z = n // (X * C)
    me, cy = lax.axis_index("rows"), lax.axis_index("cols")
    z, x, c = lax.div(me, X * C), lax.rem(lax.div(me, C), X), lax.rem(me, C)
    ntc = nt // tile_sem.shape[0]
    far = sorted(range(Z), key=lambda d: -min(d, Z - d))
    groups = X * C

    def steps(g):
        return X - 1 - lax.rem(g, X), C - 1 - lax.div(g, X)

    loads = [
        pltpu.make_async_copy(
            tiles_hbm.at[pl.ds(i * ntc, ntc)], tiles.at[pl.ds(i * ntc, ntc)], tile_sem.at[i]
        )
        for i in range(tile_sem.shape[0])
    ]
    bring = pltpu.make_async_copy(vec_hbm, vec_ref, vec_sem)
    bring.start()
    pairs_in = ((send_hbm, send_ref), (row_hbm, row_ref), (src_hbm, src_ref), (ritz_hbm, ritz_ref))
    smalls = [pltpu.make_async_copy(a, b, small_sem.at[i]) for i, (a, b) in enumerate(pairs_in)]
    for small in smalls:
        small.start()
    to_z = [lax.rem(z + d, Z) * groups for d in far]
    from_z = [lax.rem(z - d + Z, Z) * groups for d in far]

    barrier = pltpu.get_barrier_semaphore()

    def each_peer(act):
        def plane(g, carry, count=Z):
            dx, dc = steps(g)
            rest = lax.rem(x + dx, X) * C + lax.rem(c + dc, C)
            for j in range(count):
                act(g * Z + j, to_z[j] + rest)
            return carry

        lax.fori_loop(0, groups - 1, plane, 0)
        plane(groups - 1, 0, Z - 1)

    each_peer(
        lambda k, dest: pl.semaphore_signal(
            barrier, inc=1, device_id={"rows": dest}, device_id_type=MESH
        )
    )
    for d in range(1, ny):
        pl.semaphore_signal(
            barrier, inc=1, device_id={"cols": lax.rem(cy + d, ny)}, device_id_type=MESH
        )

    def unpack(r):
        both = vec_ref[:, pl.ds(pl.multiple_of(r * 256, 256), 256)].astype(F32)
        cur[0, 0, r] = both[:HV]
        cur[0, 1, r] = both[HV:]

    bring.wait()
    for small in smalls:
        small.wait()
    for load in loads:
        load.start()
    unrolled(nb, 8, unpack)

    def chosen(side, h, dest):
        return jnp.concatenate(
            [cur[side, h, send_ref[0, dest]], cur[side, h, send_ref[1, dest]]], axis=0
        ).astype(BF16)

    def pack(p, h):
        side = p % 2
        land[p, h, n - 1] = chosen(side, h, me)

        def step(k, dest):
            outb[p, h, k] = chosen(side, h, dest)

        each_peer(step)

    def message(p, h, k, dest):
        return pltpu.make_async_remote_copy(
            src_ref=outb.at[p, h, k], dst_ref=land.at[p, h, k],
            send_sem=ssem.at[p, h], recv_sem=rsem.at[p, h, lax.div(k, Z)],
            device_id={"rows": dest}, device_id_type=MESH,
        )

    def send(p, h):
        each_peer(lambda k, dest: message(p, h, k, dest).start())

    def many(p, h, g, first, count):
        at = pl.ds(first, count)
        return pltpu.make_async_remote_copy(
            src_ref=outb.at[p, h, at], dst_ref=land.at[p, h, at],
            send_sem=ssem.at[p, h], recv_sem=rsem.at[p, h, g],
            device_id={"rows": lax.rem(me + 1, n)}, device_id_type=MESH,
        )

    def product(rows, tile):
        return lax.dot_general(
            rows, tiles[tile], (((1,), (0,)), ((), ())), preferred_element_type=F32
        )

    def own_products(p, h):
        def step(s):
            prods[h, s] = product(cur[p % 2, h, s].astype(BF16), index_s[0, s])

        unrolled(nb, 8, step)

    def received_products(p, h, g, count=Z):
        many(p, h, g, g * Z, count).wait_recv()
        dx, dc = steps(g)
        rest = lax.rem(x - dx + X, X) * C + lax.rem(c - dc + C, C)
        for j in range(Z):
            s = nb + 2 * (from_z[j] + rest)
            block = land[p, h, g * Z + j]
            prods[h, s] = product(block, index_s[0, s])[:HV]
            prods[h, s + 1] = product(block, index_s[0, s + 1])[HV:]

    def add(h, first, count):
        def step(i, total):
            for u in range(8):
                k = first + i * 8 + u
                total = total * same_s[0, k] + prods[h, index_s[1, k]]
                accs[k] = total
            return total

        lax.fori_loop(0, count // 8, step, jnp.zeros((HV, 256), F32))

    def apply(p, h):
        def step(g, carry):
            received_products(p, h, g)
            return carry

        lax.fori_loop(0, groups // 2, step, 0)
        add(h, 0, nb + n)
        lax.fori_loop(groups // 2, groups - 1, step, 0)
        received_products(p, h, groups - 1, Z - 1)
        add(h, nb + n, n)

    def summed(r):
        return accs[index_s[2, r]] + accs[index_s[2, nb + r]]

    def pairs(emit):
        unrolled(nb // 2, 4, lambda i: emit(i, summed(2 * i), summed(2 * i + 1)))

    def across(h, d):
        return pltpu.make_async_remote_copy(
            src_ref=full.at[cy, h], dst_ref=full.at[cy, h],
            send_sem=ysend.at[h, d - 1], recv_sem=yrecv.at[h, d - 1],
            device_id={"cols": lax.rem(cy + d, ny)}, device_id_type=MESH,
        )

    def across_arrival(h, d):
        slot = lax.rem(cy - d + ny, ny)
        return pltpu.make_async_remote_copy(
            src_ref=full.at[slot, h], dst_ref=full.at[slot, h],
            send_sem=ysend.at[h, d - 1], recv_sem=yrecv.at[h, d - 1],
            device_id={"cols": lax.rem(cy + d, ny)}, device_id_type=MESH,
        )

    accs[nt] = jnp.zeros((HV, 256), F32)
    pack(0, 0)
    pl.semaphore_wait(barrier, n - 1 + ny - 1)
    send(0, 0)
    pack(0, 1)
    send(0, 1)

    side = (nt, nt)
    down = lax.broadcasted_iota(jnp.int32, side, 0)
    along = lax.broadcasted_iota(jnp.int32, side, 1)

    def upright(line):
        spread = jnp.where(down == along, jnp.broadcast_to(line, side).astype(F32), 0.0)
        return jnp.sum(spread, axis=1, keepdims=True).astype(jnp.int32)

    def gather(where, value):
        return jnp.sum(jnp.where(where, value, 0), axis=0, keepdims=True)

    src = src_ref[...]
    late = (src >= nb) & (lax.rem(lax.div(src - nb, 2), C) == c)
    row = row_ref[...] + jnp.where(late, nb, 0)
    row_c, src_c = upright(row), upright(src)
    key = row * nt + lax.broadcasted_iota(jnp.int32, (1, nt), 1)
    key_c = row_c * nt + lax.broadcasted_iota(jnp.int32, (nt, 1), 0)
    rank_c = jnp.sum(
        jnp.where(key < key_c, 1.0, 0.0).astype(F32), axis=1, keepdims=True
    ).astype(jnp.int32)
    placed = rank_c == along
    index_v[0:1, :nt] = gather(src_c == along, down)
    index_v[1:2, :nt] = gather(placed, src_c)
    upto = gather(row_c <= along, 1)
    under = gather(row_c < along, 1)
    index_v[2:3, :nt] = jnp.where(upto > under, upto - 1, nt)
    same_v[0:1, :nt] = jnp.where(
        gather(placed, row_c) + 1 == gather(rank_c + 1 == along, row_c + 1), 1.0, 0.0
    )
    moves = [
        pltpu.make_async_copy(index_v, index_s, index_sem.at[0]),
        pltpu.make_async_copy(same_v, same_s, index_sem.at[1]),
    ]
    for move in moves:
        move.start()
    for i, load in enumerate(loads):
        load.wait()

        def flip(j, i=i):
            t = i * ntc + j
            tiles[t] = tiles[t].T

        unrolled(ntc, 4, flip)
    for move in moves:
        move.wait()
    own_products(0, 0)
    own_products(0, 1)

    def first(h):
        def emit(i, a, b):
            cur[1, h, 2 * i] = a.astype(BF16).astype(F32)
            cur[1, h, 2 * i + 1] = b.astype(BF16).astype(F32)

        return emit

    def second(h):
        def emit(i, a, b):
            old = vec_ref[:, pl.ds(pl.multiple_of(i * 512, 512), 512)].astype(F32)
            old = old[h * HV : (h + 1) * HV]
            both = jnp.concatenate([2.0 * a - old[:, :256], 2.0 * b - old[:, 256:]], axis=0)
            both = both.astype(BF16)
            full[cy, h, i] = both
            both = both.astype(F32)
            cur[0, h, 2 * i] = both[:HV]
            cur[0, h, 2 * i + 1] = both[HV:]

        return emit

    def third(i, a, b):
        opb[i] = jnp.concatenate([a, b], axis=0).astype(BF16)

    for p, maker in ((0, first), (1, second)):
        for h in (0, 1):
            apply(p, h)
            pairs(maker(h))
            pack(p + 1, h)
            send(p + 1, h)
            if p == 1:
                for d in range(1, ny):
                    across(h, d).start()
            own_products(p + 1, h)

    apply(2, 0)
    pairs(third)

    wide = ny * 2 * 2 * HV
    narrow = ny * 2 * HV
    column = lax.broadcasted_iota(jnp.int32, (narrow, wide), 1)
    vector = lax.broadcasted_iota(jnp.int32, (narrow, wide), 0)
    matches = lax.div(column, 32) * 16 + lax.rem(lax.div(column, 16), 2) * 8 + lax.rem(column, 8) == vector
    parity = lax.rem(lax.div(column, 8), 2)
    turns = [
        lax.dot_general(
            ritz_ref[...], jnp.where(matches & (parity == q), 1.0, 0.0).astype(BF16),
            (((1,), (0,)), ((), ())), preferred_element_type=F32,
        )
        for q in (0, 1)
    ]
    turn = jnp.concatenate(turns, axis=0).astype(BF16)

    apply(2, 1)

    for h in (0, 1):
        for d in range(1, ny):
            across_arrival(h, d).wait_recv()

    def weights(i):
        return full[:, :, i].reshape(wide, 256)

    def contract(j, total):
        for u in range(4):
            i = j * 4 + u
            rest = jnp.concatenate([summed(2 * i), summed(2 * i + 1)], axis=0).astype(BF16)
            rows = jnp.concatenate([full[cy, 0, i], full[cy, 1, i], opb[i], rest], axis=0)
            total = total + lax.dot_general(
                rows, weights(i), (((1,), (1,)), ((), ())), preferred_element_type=F32
            )
        return total

    sums = lax.fori_loop(0, nb // 8, contract, jnp.zeros((8 * HV, wide), F32))

    def rotate():
        def step(i):
            turned = jnp.dot(turn, weights(i), preferred_element_type=F32).astype(BF16)
            at = pl.multiple_of(i * 512, 512)
            rot_ref[:, pl.ds(at, 256)] = turned[: 2 * HV]
            rot_ref[:, pl.ds(at + 256, 256)] = turned[2 * HV :]

        unrolled(nb // 2, 4, step)

    sums = sums.reshape(4, 2, HV, wide)
    even, odd = sums[:, 0].reshape(4 * HV, wide), sums[:, 1].reshape(4 * HV, wide)
    first = lax.rem(lax.div(lax.broadcasted_iota(jnp.int32, (2 * HV, wide), 1), HV), 2) == 0
    mine = jnp.where(
        first,
        even[: 2 * HV] + pltpu.roll(odd[: 2 * HV], wide - HV, 1),
        odd[2 * HV :] + pltpu.roll(even[2 * HV :], HV, 1),
    )

    def reduce(stage, red, mine, position, count, to, meanwhile):
        red[position] = mine

        def copies(d, slot):
            return pltpu.make_async_remote_copy(
                src_ref=red.at[slot], dst_ref=red.at[slot],
                send_sem=qsend.at[stage, d - 1], recv_sem=qrecv.at[stage, d - 1],
                device_id={"rows": to(d)}, device_id_type=MESH,
            )

        for d in range(1, count):
            copies(d, position).start()
        meanwhile()
        for d in range(1, count):
            copies(d, lax.rem(position - d + count, count)).wait_recv()
        total = red[0]
        for d in range(1, count):
            total = total + red[d]
        for d in range(1, count):
            copies(d, position).wait_send()
        return total

    plane = X * C
    spot = lax.rem(me, plane)
    mine = reduce(0, red1, mine, spot, plane, lambda d: z * plane + lax.rem(spot + d, plane), rotate)
    mine = reduce(1, red2, mine, z, Z, lambda d: lax.rem(z + d, Z) * plane + spot, lambda: None)
    mine = mine * (1.0 / total_nodes)
    sums_ref[...] = mine
    for p in range(3):
        for h in (0, 1):
            many(p, h, 0, 0, n - 1).wait_send()
    for h in (0, 1):
        for d in range(1, ny):
            across(h, d).wait_send()


def finish(rot_ref, sums_ref, rotated_hbm, gram_hbm, projected_hbm, gram_ref, projected_ref, sem, out_sem):
    rows = rot_ref.shape[1] // sem.shape[0]
    copies = [
        pltpu.make_async_copy(
            rot_ref.at[:, pl.ds(i * rows, rows)], rotated_hbm.at[:, pl.ds(i * rows, rows)], sem.at[i]
        )
        for i in range(sem.shape[0])
    ]
    for copy in copies:
        copy.start()
    wide, k = sums_ref.shape[1], gram_ref.shape[1]
    column = lax.broadcasted_iota(jnp.int32, (wide, k), 0)
    vector = lax.broadcasted_iota(jnp.int32, (wide, k), 1)
    place = lax.div(column, 2 * HV) * HV + lax.rem(column, HV) == vector
    parity = lax.rem(lax.div(column, HV), 2)
    for q, out_ref in ((0, gram_ref), (1, projected_ref)):
        out_ref[...] = jnp.dot(
            sums_ref[...], jnp.where(place & (parity == q), 1.0, 0.0).astype(F32),
            precision=lax.Precision.HIGHEST, preferred_element_type=F32,
        )
    for i, (a, b) in enumerate(((gram_ref, gram_hbm), (projected_ref, projected_hbm))):
        copies.append(pltpu.make_async_copy(a, b, out_sem.at[i]))
        copies[-1].start()
    for copy in copies:
        copy.wait()


def solution(mesh):
    n, ny = mesh.shape["rows"], mesh.shape["cols"]

    def body(vectors, tile_vals, tile_row, tile_src, send_list, ritz):
        nt = tile_vals.shape[0]
        nb = vectors.shape[1] // 256
        k = ritz.shape[0]
        vmem = pl.BlockSpec(memory_space=pltpu.VMEM)
        dma = pltpu.SemaphoreType.DMA
        anywhere = pl.BlockSpec(memory_space=pl.ANY)
        rotated, sums = pl.pallas_call(
            functools.partial(kernel, n, ny, nb, nt, vectors.shape[1] * n),
            out_shape=(
                pltpu.VMEM(vectors.shape, BF16),
                pltpu.VMEM((2 * HV, 2 * k), F32),
            ),
            in_specs=[anywhere] * 6,
            out_specs=(vmem, vmem),
            scratch_shapes=[
                pltpu.VMEM(tile_row.shape, jnp.int32),
                pltpu.VMEM(tile_src.shape, jnp.int32),
                pltpu.SMEM(send_list.shape[::-1], jnp.int32),
                pltpu.VMEM(ritz.shape[::-1], BF16),
                pltpu.VMEM(vectors.shape, BF16),
                pltpu.VMEM((nt, 256, 256), BF16),
                pltpu.VMEM((2, 2, nb, HV, 256), F32),
                pltpu.VMEM((3, 2, n, 2 * HV, 256), BF16),
                pltpu.VMEM((3, 2, n, 2 * HV, 256), BF16),
                pltpu.VMEM((2, nt, HV, 256), F32),
                pltpu.VMEM((nt + 1, HV, 256), F32),
                pltpu.VMEM((nb // 2, 2 * HV, 256), BF16),
                pltpu.VMEM((ny, 2, nb // 2, 2 * HV, 256), BF16),
                pltpu.VMEM((X * C, 2 * HV, 2 * k), F32),
                pltpu.VMEM((n // (X * C), 2 * HV, 2 * k), F32),
                pltpu.VMEM((8, 256), jnp.int32),
                pltpu.VMEM((8, 256), F32),
                pltpu.SMEM((8, 256), jnp.int32),
                pltpu.SMEM((8, 256), F32),
                dma((4,)),
                dma,
                dma((2,)),
                dma((8,)),
                dma((3, 2)),
                dma((3, 2, X * C)),
                dma((2, ny - 1)),
                dma((2, ny - 1)),
                dma((2, 7)),
                dma((2, 7)),
            ],
            compiler_params=pltpu.CompilerParams(
                collective_id=0, has_side_effects=True, vmem_limit_bytes=56 << 20
            ),
        )(tile_row, tile_src, send_list.T, ritz.T, vectors, tile_vals)
        return pl.pallas_call(
            finish,
            out_shape=(
                jax.ShapeDtypeStruct(vectors.shape, BF16),
                jax.ShapeDtypeStruct((2 * HV, k), F32),
                jax.ShapeDtypeStruct((2 * HV, k), F32),
            ),
            in_specs=[vmem, vmem],
            out_specs=(anywhere, anywhere, anywhere),
            scratch_shapes=[
                pltpu.VMEM((2 * HV, k), F32),
                pltpu.VMEM((2 * HV, k), F32),
                dma((4,)),
                dma((2,)),
            ],
            compiler_params=pltpu.CompilerParams(vmem_limit_bytes=4 << 20),
        )(rotated, sums)

    return jax.shard_map(
        body,
        mesh=mesh,
        in_specs=(
            P("cols", "rows"),
            P("rows", None, None),
            P("rows", None),
            P("rows", None),
            P("rows", None),
            P(None, "cols"),
        ),
        out_specs=(P("cols", "rows"), P("cols", None), P("cols", None)),
        check_vma=False,
    )
```

```python
import functools

import jax
import jax.numpy as jnp
from jax import lax
from jax.experimental import pallas as pl
from jax.experimental.pallas import tpu as pltpu
from jax.sharding import PartitionSpec as P

MESH = pl.DeviceIdType.MESH
F32, BF16 = jnp.float32, jnp.bfloat16
X, C = 4, 2
HV = 8


def unrolled(count, unroll, step):
    assert count % unroll == 0

    def body(i, carry):
        for u in range(unroll):
            step(i * unroll + u)
        return carry

    lax.fori_loop(0, count // unroll, body, 0)


def kernel(
    n, ny, nb, nt, total_nodes,
    row_hbm, src_hbm, send_hbm, ritz_hbm, vec_hbm, tiles_hbm,
    rot_ref, sums_ref,
    row_ref, src_ref, send_ref, ritz_ref, vec_ref, tiles, cur, outb, land, prods, accs, opb, full, red1, red2,
    index_v, same_v, index_s, same_s,
    small_sem, vec_sem, index_sem, tile_sem, ssem, rsem, ysend, yrecv, qsend, qrecv,
):
    Z = n // (X * C)
    me, cy = lax.axis_index("rows"), lax.axis_index("cols")
    z, x, c = lax.div(me, X * C), lax.rem(lax.div(me, C), X), lax.rem(me, C)
    ntc = nt // tile_sem.shape[0]
    far = sorted(range(Z), key=lambda d: -min(d, Z - d))
    groups = X * C

    def steps(g):
        return X - 1 - lax.rem(g, X), C - 1 - lax.div(g, X)

    loads = [
        pltpu.make_async_copy(
            tiles_hbm.at[pl.ds(i * ntc, ntc)], tiles.at[pl.ds(i * ntc, ntc)], tile_sem.at[i]
        )
        for i in range(tile_sem.shape[0])
    ]
    bring = pltpu.make_async_copy(vec_hbm, vec_ref, vec_sem)
    bring.start()
    pairs_in = ((send_hbm, send_ref), (row_hbm, row_ref), (src_hbm, src_ref), (ritz_hbm, ritz_ref))
    smalls = [pltpu.make_async_copy(a, b, small_sem.at[i]) for i, (a, b) in enumerate(pairs_in)]
    for small in smalls:
        small.start()
    to_z = [lax.rem(z + d, Z) * groups for d in far]
    from_z = [lax.rem(z - d + Z, Z) * groups for d in far]

    barrier = pltpu.get_barrier_semaphore()

    def each_peer(act):
        def plane(g, carry, count=Z):
            dx, dc = steps(g)
            rest = lax.rem(x + dx, X) * C + lax.rem(c + dc, C)
            for j in range(count):
                act(g * Z + j, to_z[j] + rest)
            return carry

        lax.fori_loop(0, groups - 1, plane, 0)
        plane(groups - 1, 0, Z - 1)

    each_peer(
        lambda k, dest: pl.semaphore_signal(
            barrier, inc=1, device_id={"rows": dest}, device_id_type=MESH
        )
    )
    for d in range(1, ny):
        pl.semaphore_signal(
            barrier, inc=1, device_id={"cols": lax.rem(cy + d, ny)}, device_id_type=MESH
        )

    def unpack(r):
        both = vec_ref[:, pl.ds(pl.multiple_of(r * 256, 256), 256)].astype(F32)
        cur[0, 0, r] = both[:HV]
        cur[0, 1, r] = both[HV:]

    bring.wait()
    for small in smalls:
        small.wait()
    for load in loads:
        load.start()
    unrolled(nb, 8, unpack)

    def chosen(side, h, dest):
        return jnp.concatenate(
            [cur[side, h, send_ref[0, dest]], cur[side, h, send_ref[1, dest]]], axis=0
        ).astype(BF16)

    def pack(p, h):
        side = p % 2
        land[p, h, n - 1] = chosen(side, h, me)

        def step(k, dest):
            outb[p, h, k] = chosen(side, h, dest)
            message(p, h, k, dest).start()

        each_peer(step)

    def message(p, h, k, dest):
        return pltpu.make_async_remote_copy(
            src_ref=outb.at[p, h, k], dst_ref=land.at[p, h, k],
            send_sem=ssem.at[p, h], recv_sem=rsem.at[p, h, lax.div(k, Z)],
            device_id={"rows": dest}, device_id_type=MESH,
        )

    def many(p, h, g, first, count):
        at = pl.ds(first, count)
        return pltpu.make_async_remote_copy(
            src_ref=outb.at[p, h, at], dst_ref=land.at[p, h, at],
            send_sem=ssem.at[p, h], recv_sem=rsem.at[p, h, g],
            device_id={"rows": lax.rem(me + 1, n)}, device_id_type=MESH,
        )

    def product(rows, tile):
        return lax.dot_general(
            rows, tiles[tile], (((1,), (0,)), ((), ())), preferred_element_type=F32
        )

    def own_products(p, h):
        def step(s):
            prods[h, s] = product(cur[p % 2, h, s].astype(BF16), index_s[0, s])

        unrolled(nb, 8, step)

    def received_products(p, h, g, count=Z):
        many(p, h, g, g * Z, count).wait_recv()
        dx, dc = steps(g)
        rest = lax.rem(x - dx + X, X) * C + lax.rem(c - dc + C, C)
        for j in range(Z):
            s = nb + 2 * (from_z[j] + rest)
            block = land[p, h, g * Z + j]
            prods[h, s] = product(block, index_s[0, s])[:HV]
            prods[h, s + 1] = product(block, index_s[0, s + 1])[HV:]

    def add(h, first, count):
        def step(i, total):
            for u in range(8):
                k = first + i * 8 + u
                total = total * same_s[0, k] + prods[h, index_s[1, k]]
                accs[k] = total
            return total

        lax.fori_loop(0, count // 8, step, jnp.zeros((HV, 256), F32))

    def apply(p, h):
        def step(g, carry):
            received_products(p, h, g)
            return carry

        lax.fori_loop(0, groups // 2, step, 0)
        add(h, 0, nb + n)
        lax.fori_loop(groups // 2, groups - 1, step, 0)
        received_products(p, h, groups - 1, Z - 1)
        add(h, nb + n, n)

    def summed(r):
        return accs[index_s[2, r]] + accs[index_s[2, nb + r]]

    def pairs(emit):
        unrolled(nb // 2, 4, lambda i: emit(i, summed(2 * i), summed(2 * i + 1)))

    def across(h, d):
        return pltpu.make_async_remote_copy(
            src_ref=full.at[cy, h], dst_ref=full.at[cy, h],
            send_sem=ysend.at[h, d - 1], recv_sem=yrecv.at[h, d - 1],
            device_id={"cols": lax.rem(cy + d, ny)}, device_id_type=MESH,
        )

    def across_arrival(h, d):
        slot = lax.rem(cy - d + ny, ny)
        return pltpu.make_async_remote_copy(
            src_ref=full.at[slot, h], dst_ref=full.at[slot, h],
            send_sem=ysend.at[h, d - 1], recv_sem=yrecv.at[h, d - 1],
            device_id={"cols": lax.rem(cy + d, ny)}, device_id_type=MESH,
        )

    accs[nt] = jnp.zeros((HV, 256), F32)
    pl.semaphore_wait(barrier, n - 1 + ny - 1)
    pack(0, 0)
    pack(0, 1)

    side = (nt, nt)
    down = lax.broadcasted_iota(jnp.int32, side, 0)
    along = lax.broadcasted_iota(jnp.int32, side, 1)

    def upright(line):
        spread = jnp.where(down == along, jnp.broadcast_to(line, side).astype(F32), 0.0)
        return jnp.sum(spread, axis=1, keepdims=True).astype(jnp.int32)

    def gather(where, value):
        return jnp.sum(jnp.where(where, value, 0), axis=0, keepdims=True)

    src = src_ref[...]
    late = (src >= nb) & (lax.rem(lax.div(src - nb, 2), C) == c)
    row = row_ref[...] + jnp.where(late, nb, 0)
    row_c, src_c = upright(row), upright(src)
    key = row * nt + lax.broadcasted_iota(jnp.int32, (1, nt), 1)
    key_c = row_c * nt + lax.broadcasted_iota(jnp.int32, (nt, 1), 0)
    rank_c = jnp.sum(
        jnp.where(key < key_c, 1.0, 0.0).astype(F32), axis=1, keepdims=True
    ).astype(jnp.int32)
    placed = rank_c == along
    index_v[0:1, :nt] = gather(src_c == along, down)
    index_v[1:2, :nt] = gather(placed, src_c)
    upto = gather(row_c <= along, 1)
    under = gather(row_c < along, 1)
    index_v[2:3, :nt] = jnp.where(upto > under, upto - 1, nt)
    same_v[0:1, :nt] = jnp.where(
        gather(placed, row_c) + 1 == gather(rank_c + 1 == along, row_c + 1), 1.0, 0.0
    )
    moves = [
        pltpu.make_async_copy(index_v, index_s, index_sem.at[0]),
        pltpu.make_async_copy(same_v, same_s, index_sem.at[1]),
    ]
    for move in moves:
        move.start()
    for i, load in enumerate(loads):
        load.wait()

        def flip(j, i=i):
            t = i * ntc + j
            tiles[t] = tiles[t].T

        unrolled(ntc, 4, flip)
    for move in moves:
        move.wait()
    own_products(0, 0)
    own_products(0, 1)

    def first(h):
        def emit(i, a, b):
            cur[1, h, 2 * i] = a.astype(BF16).astype(F32)
            cur[1, h, 2 * i + 1] = b.astype(BF16).astype(F32)

        return emit

    def second(h):
        def emit(i, a, b):
            old = vec_ref[:, pl.ds(pl.multiple_of(i * 512, 512), 512)].astype(F32)
            old = old[h * HV : (h + 1) * HV]
            both = jnp.concatenate([2.0 * a - old[:, :256], 2.0 * b - old[:, 256:]], axis=0)
            both = both.astype(BF16)
            full[cy, h, i] = both
            both = both.astype(F32)
            cur[0, h, 2 * i] = both[:HV]
            cur[0, h, 2 * i + 1] = both[HV:]

        return emit

    def third(i, a, b):
        opb[i] = jnp.concatenate([a, b], axis=0).astype(BF16)

    for p, maker in ((0, first), (1, second)):
        for h in (0, 1):
            apply(p, h)
            pairs(maker(h))
            pack(p + 1, h)
            if p == 1:
                for d in range(1, ny):
                    across(h, d).start()
            own_products(p + 1, h)

    apply(2, 0)
    pairs(third)

    wide = ny * 2 * 2 * HV
    narrow = ny * 2 * HV
    column = lax.broadcasted_iota(jnp.int32, (narrow, wide), 1)
    vector = lax.broadcasted_iota(jnp.int32, (narrow, wide), 0)
    matches = lax.div(column, 32) * 16 + lax.rem(lax.div(column, 16), 2) * 8 + lax.rem(column, 8) == vector
    parity = lax.rem(lax.div(column, 8), 2)
    turns = [
        lax.dot_general(
            ritz_ref[...], jnp.where(matches & (parity == q), 1.0, 0.0).astype(BF16),
            (((1,), (0,)), ((), ())), preferred_element_type=F32,
        )
        for q in (0, 1)
    ]
    turn = jnp.concatenate(turns, axis=0).astype(BF16)

    apply(2, 1)

    for h in (0, 1):
        for d in range(1, ny):
            across_arrival(h, d).wait_recv()

    def weights(i):
        return full[:, :, i].reshape(wide, 256)

    def contract(j, total):
        for u in range(4):
            i = j * 4 + u
            rest = jnp.concatenate([summed(2 * i), summed(2 * i + 1)], axis=0).astype(BF16)
            rows = jnp.concatenate([full[cy, 0, i], full[cy, 1, i], opb[i], rest], axis=0)
            total = total + lax.dot_general(
                weights(i), rows, (((1,), (1,)), ((), ())), preferred_element_type=F32
            )
        return total

    sums = lax.fori_loop(0, nb // 8, contract, jnp.zeros((wide, 8 * HV), F32)).T

    def rotate():
        def step(i):
            turned = jnp.dot(turn, weights(i), preferred_element_type=F32).astype(BF16)
            at = pl.multiple_of(i * 512, 512)
            rot_ref[:, pl.ds(at, 256)] = turned[: 2 * HV]
            rot_ref[:, pl.ds(at + 256, 256)] = turned[2 * HV :]

        unrolled(nb // 2, 4, step)

    sums = sums.reshape(4, 2, HV, wide)
    even, odd = sums[:, 0].reshape(4 * HV, wide), sums[:, 1].reshape(4 * HV, wide)
    first = lax.rem(lax.div(lax.broadcasted_iota(jnp.int32, (2 * HV, wide), 1), HV), 2) == 0
    mine = jnp.where(
        first,
        even[: 2 * HV] + pltpu.roll(odd[: 2 * HV], wide - HV, 1),
        odd[2 * HV :] + pltpu.roll(even[2 * HV :], HV, 1),
    )

    def reduce(stage, red, mine, position, count, to, meanwhile):
        red[position] = mine

        def copies(d, slot):
            return pltpu.make_async_remote_copy(
                src_ref=red.at[slot], dst_ref=red.at[slot],
                send_sem=qsend.at[stage, d - 1], recv_sem=qrecv.at[stage, d - 1],
                device_id={"rows": to(d)}, device_id_type=MESH,
            )

        for d in range(1, count):
            copies(d, position).start()
        meanwhile()
        for d in range(1, count):
            copies(d, lax.rem(position - d + count, count)).wait_recv()
        total = red[0]
        for d in range(1, count):
            total = total + red[d]
        for d in range(1, count):
            copies(d, position).wait_send()
        return total

    plane = X * C
    spot = lax.rem(me, plane)
    mine = reduce(0, red1, mine, spot, plane, lambda d: z * plane + lax.rem(spot + d, plane), lambda: None)
    mine = reduce(1, red2, mine, z, Z, lambda d: lax.rem(z + d, Z) * plane + spot, rotate)
    mine = mine * (1.0 / total_nodes)
    sums_ref[...] = mine
    for p in range(3):
        for h in (0, 1):
            many(p, h, 0, 0, n - 1).wait_send()
    for h in (0, 1):
        for d in range(1, ny):
            across(h, d).wait_send()


def finish(rot_ref, sums_ref, rotated_hbm, gram_hbm, projected_hbm, gram_ref, projected_ref, sem, out_sem):
    rows = rot_ref.shape[1] // sem.shape[0]
    copies = [
        pltpu.make_async_copy(
            rot_ref.at[:, pl.ds(i * rows, rows)], rotated_hbm.at[:, pl.ds(i * rows, rows)], sem.at[i]
        )
        for i in range(sem.shape[0])
    ]
    for copy in copies:
        copy.start()
    wide, k = sums_ref.shape[1], gram_ref.shape[1]
    column = lax.broadcasted_iota(jnp.int32, (wide, k), 0)
    vector = lax.broadcasted_iota(jnp.int32, (wide, k), 1)
    place = lax.div(column, 2 * HV) * HV + lax.rem(column, HV) == vector
    parity = lax.rem(lax.div(column, HV), 2)
    for q, out_ref in ((0, gram_ref), (1, projected_ref)):
        out_ref[...] = jnp.dot(
            sums_ref[...], jnp.where(place & (parity == q), 1.0, 0.0).astype(F32),
            precision=lax.Precision.HIGHEST, preferred_element_type=F32,
        )
    for i, (a, b) in enumerate(((gram_ref, gram_hbm), (projected_ref, projected_hbm))):
        copies.append(pltpu.make_async_copy(a, b, out_sem.at[i]))
        copies[-1].start()
    for copy in copies:
        copy.wait()


def solution(mesh):
    n, ny = mesh.shape["rows"], mesh.shape["cols"]

    def body(vectors, tile_vals, tile_row, tile_src, send_list, ritz):
        nt = tile_vals.shape[0]
        nb = vectors.shape[1] // 256
        k = ritz.shape[0]
        vmem = pl.BlockSpec(memory_space=pltpu.VMEM)
        dma = pltpu.SemaphoreType.DMA
        anywhere = pl.BlockSpec(memory_space=pl.ANY)
        rotated, sums = pl.pallas_call(
            functools.partial(kernel, n, ny, nb, nt, vectors.shape[1] * n),
            out_shape=(
                pltpu.VMEM(vectors.shape, BF16),
                pltpu.VMEM((2 * HV, 2 * k), F32),
            ),
            in_specs=[anywhere] * 6,
            out_specs=(vmem, vmem),
            scratch_shapes=[
                pltpu.VMEM(tile_row.shape, jnp.int32),
                pltpu.VMEM(tile_src.shape, jnp.int32),
                pltpu.SMEM(send_list.shape[::-1], jnp.int32),
                pltpu.VMEM(ritz.shape[::-1], BF16),
                pltpu.VMEM(vectors.shape, BF16),
                pltpu.VMEM((nt, 256, 256), BF16),
                pltpu.VMEM((2, 2, nb, HV, 256), F32),
                pltpu.VMEM((3, 2, n, 2 * HV, 256), BF16),
                pltpu.VMEM((3, 2, n, 2 * HV, 256), BF16),
                pltpu.VMEM((2, nt, HV, 256), F32),
                pltpu.VMEM((nt + 1, HV, 256), F32),
                pltpu.VMEM((nb // 2, 2 * HV, 256), BF16),
                pltpu.VMEM((ny, 2, nb // 2, 2 * HV, 256), BF16),
                pltpu.VMEM((X * C, 2 * HV, 2 * k), F32),
                pltpu.VMEM((n // (X * C), 2 * HV, 2 * k), F32),
                pltpu.VMEM((8, 256), jnp.int32),
                pltpu.VMEM((8, 256), F32),
                pltpu.SMEM((8, 256), jnp.int32),
                pltpu.SMEM((8, 256), F32),
                dma((4,)),
                dma,
                dma((2,)),
                dma((8,)),
                dma((3, 2)),
                dma((3, 2, X * C)),
                dma((2, ny - 1)),
                dma((2, ny - 1)),
                dma((2, 7)),
                dma((2, 7)),
            ],
            compiler_params=pltpu.CompilerParams(
                collective_id=0, has_side_effects=True, vmem_limit_bytes=56 << 20
            ),
        )(tile_row, tile_src, send_list.T, ritz.T, vectors, tile_vals)
        return pl.pallas_call(
            finish,
            out_shape=(
                jax.ShapeDtypeStruct(vectors.shape, BF16),
                jax.ShapeDtypeStruct((2 * HV, k), F32),
                jax.ShapeDtypeStruct((2 * HV, k), F32),
            ),
            in_specs=[vmem, vmem],
            out_specs=(anywhere, anywhere, anywhere),
            scratch_shapes=[
                pltpu.VMEM((2 * HV, k), F32),
                pltpu.VMEM((2 * HV, k), F32),
                dma((4,)),
                dma((2,)),
            ],
            compiler_params=pltpu.CompilerParams(vmem_limit_bytes=4 << 20),
        )(rotated, sums)

    return jax.shard_map(
        body,
        mesh=mesh,
        in_specs=(
            P("cols", "rows"),
            P("rows", None, None),
            P("rows", None),
            P("rows", None),
            P("rows", None),
            P(None, "cols"),
        ),
        out_specs=(P("cols", "rows"), P("cols", None), P("cols", None)),
        check_vma=False,
    )
```
